32 devices in a mesh: dp: 2 (over core), ctx: 4 (over y, x), head: 4 (over z).
Axes of the slice: x: 2, y: 2, z: 4, core: 2. Of those that a mesh axis runs over, the one named last changes fastest.
Arguments:
- value_input: bfloat16 [2, 2048, 8192], P('dp', 'ctx', 'head'), may hold values from -6 to 6
- state_proj: bfloat16 [2, 2048, 256], P('dp', 'ctx'), may hold values from -6 to 6
- step_raw: float32 [2, 128, 2048], P('dp', 'head', 'ctx'), may hold values from -4 to 10
- doc_lengths: int32 [2, 8], P('dp'), may hold values from 1 to 1024, 2048 in all within a row
- conv_value: float32 [4, 8192], P(None, 'head'), may hold values from -2 to 2
- conv_state: float32 [4, 256], replicated, may hold values from -2 to 2
- step_bias: float32 [128], P('head'), may hold values from -8 to -3.5
- decay_log: float32 [128], P('head'), may hold values from -1.5 to 1
- skip_gain: float32 [128], P('head'), may hold values from 0.2 to 1
- out_grad: bfloat16 [2, 2048, 8192], P('dp', 'ctx', 'head'), may hold values from -6 to 6
Outputs:
- mixed_out: bfloat16 [2, 2048, 8192], P('dp', 'ctx', 'head')
- value_grad: bfloat16 [2, 2048, 8192], P('dp', 'ctx', 'head')
- state_grad: bfloat16 [2, 2048, 256], P('dp', 'ctx')
- step_grad: float32 [2, 128, 2048], P('dp', 'head', 'ctx')
- conv_value_grad: float32 [4, 8192], P(None, 'head')
- conv_state_grad: float32 [4, 256], replicated
- head_grads: float32 [3, 128], P(None, 'head')
The draws below stay inside these ranges and needn't reach their ends.
Inputs may be any that keep to these rules, and one draw needn't show every extreme that they name: `doc_lengths`: each row sums to 2048; its longest document has 1024 tokens.
All inputs are finite; a program needn't handle non-finite values.
Results may differ from the reference program's by a relative error of at most 0.001.
Values may be sent and summed in bfloat16 or wider, within the bound.
A program may use at most 128 MiB of HBM per device.

```python
import math
from functools import partial
import jax
import jax.numpy as jnp
import numpy as np
from jax import lax

HEADS = 128
HEAD_DIM = 64
STATE = 128
KERNEL = 4
BLOCK = 256
DOCS = 8
PACK_TOTAL = 2
PACK_TOKENS = 2048


def draw_step_raw(key, part):
    key = jax.random.fold_in(key, 11)
    root_random_key, spike_random_key = jax.random.split(key)
    starting_values = jnp.clip(jax.random.normal(root_random_key, (PACK_TOTAL, HEADS, PACK_TOKENS), jnp.float32), -4.0, 4.0)
    spike_events = jax.random.randint(spike_random_key, (PACK_TOTAL, 1, PACK_TOKENS), 0, PACK_TOKENS) < 3
    return starting_values + 6.0 * spike_events.astype(jnp.float32)


def levels(key, dims, pieces, least, largest):
    def one(position, blocks):
        draws = jax.random.uniform(jax.random.fold_in(jax.random.fold_in(key, 6), position), (blocks,), jnp.float32, least / len(pieces), largest / len(pieces))
        return jnp.repeat(jnp.exp(draws), dims[position] // blocks).reshape((-1,) + (1,) * (len(dims) - position - 1))

    loudness = one(*pieces[0])
    for cut in pieces[1:]:
        loudness = loudness * one(*cut)
    return loudness


def split_up(count, total, most, skew):
    portions = [(1 << 20) // math.isqrt(rank ** skew) + 1 for rank in range(2, count + 1)]
    rest, given = total - most - (count - 1), [1] * (count - 1)
    while rest > 0:
        movable = [i for i in range(count - 1) if given[i] < most]
        mass, remaining = sum([portions[i] for i in movable]), rest
        for i in movable:
            more = min(most - given[i], max(1, remaining * portions[i] // mass), rest)
            given[i] = given[i] + more
            rest = rest - more
    return np.array([most] + given)


def uneven(own_key, amount, total, limit, lean):
    if amount == 2:
        one = jax.random.randint(own_key, (), max(1, total - limit), min(limit, total - 1) + 1)
        return jnp.stack([one, total - one])
    sizes = jnp.asarray(split_up(amount, total, limit, lean), jnp.int32)
    twos = (amount - 1) // 2
    donor, receiver = sizes[1:1 + 2 * twos:2], sizes[2:2 + 2 * twos:2]
    slack = jnp.minimum(donor - 1, limit - receiver)
    moved = jax.random.randint(jax.random.fold_in(own_key, 1), (twos,), 0, 1 << 20) % (slack + 1)
    sizes = sizes.at[1:1 + 2 * twos:2].set(donor - moved).at[2:2 + 2 * twos:2].set(receiver + moved)
    return sizes[jax.random.permutation(jax.random.fold_in(own_key, 2), amount)]


def centred(key, dims, deviation, most, pieces=(), kind=jnp.bfloat16):
    result = jax.random.normal(key, dims, jnp.float32) * deviation
    if len(pieces) > 0:
        result = levels(key, dims, pieces, -0.22, 0.18) * result
    return jnp.clip(result, min=-most, max=most).astype(kind)


def setup_inputs(seed: int = 0) -> dict:
    streams_of = jax.random.split(jax.random.key(seed), 11)
    value_input = centred(streams_of[0], (PACK_TOTAL, PACK_TOKENS, HEADS * HEAD_DIM), 1.0, 6.0, ((0, 2), (1, 4), (2, 4)))
    state_proj = centred(streams_of[1], (PACK_TOTAL, PACK_TOKENS, 2 * STATE), 1.0, 6.0, ((0, 2), (1, 4)))
    step_raw = draw_step_raw(jax.random.fold_in(streams_of[10], 71), 0)
    doc_lengths = jax.vmap(lambda own: uneven(own, DOCS, PACK_TOKENS, PACK_TOKENS // 2, 2))(jax.random.split(streams_of[3], PACK_TOTAL)).reshape((PACK_TOTAL, DOCS)).astype(jnp.int32)
    conv_value = centred(streams_of[4], (KERNEL, HEADS * HEAD_DIM), 0.5, 2.0, ((1, 4),), jnp.float32)
    conv_state = centred(streams_of[5], (KERNEL, 2 * STATE), 0.5, 2.0, (), jnp.float32)
    step_bias = jnp.clip(-8.0 + 4.5 * jax.random.uniform(streams_of[6], (HEADS,), jnp.float32) ** levels(streams_of[6], (HEADS,), ((0, 4),), -0.2, 0.2), -8.0, -3.5)
    decay_log = jnp.clip(-1.5 + 2.5 * jax.random.uniform(streams_of[7], (HEADS,), jnp.float32) ** levels(streams_of[7], (HEADS,), ((0, 4),), -0.2, 0.2), -1.5, 1.0)
    skip_gain = jnp.clip(0.2 + 0.8 * jax.random.uniform(streams_of[8], (HEADS,), jnp.float32) ** levels(streams_of[8], (HEADS,), ((0, 4),), -0.2, 0.2), 0.2, 1.0)
    out_grad = centred(streams_of[9], (PACK_TOTAL, PACK_TOKENS, HEADS * HEAD_DIM), 1.0, 6.0, ((0, 2), (1, 4), (2, 4)))
    return {"value_input": value_input, "state_proj": state_proj, "step_raw": step_raw, "doc_lengths": doc_lengths, "conv_value": conv_value, "conv_state": conv_state, "step_bias": step_bias, "decay_log": decay_log, "skip_gain": skip_gain, "out_grad": out_grad}


precise = lax.Precision.HIGHEST

def token_starts(lengths, positions):
    doc_ends = jnp.cumsum(lengths).astype(jnp.int32)
    passed = doc_ends[None, :] <= positions[:, None]
    return lax.optimization_barrier(jnp.sum(jnp.where(passed, lengths[None, :], 0), axis=1)).astype(jnp.int32)

def causal_conv(series, weights, positions, starts, rim_rows):
    padded = jnp.concatenate([rim_rows, series], axis=0)
    length = series.shape[0]
    summed = jnp.zeros(series.shape, jnp.float32)
    for offset in range(KERNEL):
        source = positions - (KERNEL - 1) + offset
        usable = (source >= starts).astype(jnp.float32)
        summed = summed + weights[offset][None, :] * padded[offset:offset + length] * usable[:, None]
    return jax.nn.silu(summed)

def block_pass(carried_in, values, write_rows, read_rows, log_decay, step_sizes, positions, starts):
    block_start = positions[0]
    cumulative = jnp.cumsum(log_decay, axis=1)
    scores = jnp.dot(read_rows, write_rows.T, precision=precise)
    allowed = (positions[None, :] <= positions[:, None]) & (positions[None, :] >= starts[:, None])
    log_gaps = jnp.where(allowed[None], cumulative[:, :, None] - cumulative[:, None, :], 0.0)
    weights = jnp.where(allowed[None], jnp.exp(log_gaps), 0.0) * scores[None] * step_sizes[:, None, :]
    within = jnp.einsum('hts,hsp->htp', weights, values, precision=precise)
    entering = jnp.exp(cumulative) * (starts < block_start).astype(jnp.float32)[None, :]
    carried = jnp.einsum('tn,hpn->htp', read_rows, carried_in, precision=precise)
    within = within + entering[:, :, None] * carried
    tail_keep = (positions >= starts[-1]).astype(jnp.float32)
    tail_weight = jnp.exp(cumulative[:, -1:] - cumulative) * tail_keep[None, :] * step_sizes
    fresh_state = jnp.einsum('hsp,sn->hpn', tail_weight[:, :, None] * values, write_rows, precision=precise)
    keep_last = jnp.exp(cumulative[:, -1]) * (starts[-1] < block_start).astype(jnp.float32)
    return (keep_last[:, None, None] * carried_in + fresh_state, within)

def run_blocks(by_head, write_rows, read_rows, log_decay, step_sizes, positions, starts):
    head_count, seq_len, head_width = by_head.shape
    blocks = seq_len // BLOCK

    def one_block(carried_in, block_index):
        block_low = block_index * BLOCK
        return block_pass(carried_in, lax.dynamic_slice_in_dim(by_head, block_low, BLOCK, 1), lax.dynamic_slice_in_dim(write_rows, block_low, BLOCK, 0), lax.dynamic_slice_in_dim(read_rows, block_low, BLOCK, 0), lax.dynamic_slice_in_dim(log_decay, block_low, BLOCK, 1), lax.dynamic_slice_in_dim(step_sizes, block_low, BLOCK, 1), lax.dynamic_slice_in_dim(positions, block_low, BLOCK, 0), lax.dynamic_slice_in_dim(starts, block_low, BLOCK, 0))
    initial = jnp.zeros((head_count, head_width, write_rows.shape[1]), jnp.float32)
    closing, outputs = lax.scan(jax.checkpoint(one_block), initial, jnp.arange(blocks, dtype=jnp.int32))
    return (outputs.transpose(1, 0, 2, 3).reshape(head_count, seq_len, head_width), closing)

def pack_forward(value_input, state_proj, step_raw, conv_value, conv_state, step_bias, decay_log, skip_gain, lengths):
    seq_len = value_input.shape[0]
    positions = jnp.arange(seq_len, dtype=jnp.int32)
    starts = token_starts(lengths, positions)
    value_rim = jnp.zeros((KERNEL - 1, value_input.shape[1]), jnp.float32)
    state_rim = jnp.zeros((KERNEL - 1, state_proj.shape[1]), jnp.float32)
    values = causal_conv(value_input, conv_value, positions, starts, value_rim)
    projected = causal_conv(state_proj, conv_state, positions, starts, state_rim)
    write_rows = projected[:, :STATE]
    read_rows = projected[:, STATE:]
    step_sizes = jax.nn.softplus(step_raw + step_bias[:, None])
    log_decay = -jnp.exp(decay_log)[:, None] * step_sizes
    head_count = step_sizes.shape[0]
    by_head = values.reshape(seq_len, head_count, HEAD_DIM).transpose(1, 0, 2)
    mixed_heads, closing = run_blocks(by_head, write_rows, read_rows, log_decay, step_sizes, positions, starts)
    mixed_heads = mixed_heads + skip_gain[:, None, None] * by_head
    return mixed_heads.transpose(1, 0, 2).reshape(seq_len, head_count * HEAD_DIM)

def reference(value_input, state_proj, step_raw, doc_lengths, conv_value, conv_state, step_bias, decay_log, skip_gain, out_grad):
    mixed_list = []
    value_list = []
    state_list = []
    step_list = []
    conv_value_total = jnp.zeros(conv_value.shape, jnp.float32)
    conv_state_total = jnp.zeros(conv_state.shape, jnp.float32)
    head_total = jnp.zeros((3, step_bias.shape[0]), jnp.float32)
    for pack_index in range(PACK_TOTAL):
        forward = partial(pack_forward, lengths=doc_lengths[pack_index])
        mixed_pack, pullback = jax.vjp(forward, value_input[pack_index].astype(jnp.float32), state_proj[pack_index].astype(jnp.float32), step_raw[pack_index], conv_value, conv_state, step_bias, decay_log, skip_gain)
        gradients = pullback(out_grad[pack_index].astype(jnp.float32))
        mixed_list.append(mixed_pack.astype(jnp.bfloat16))
        value_list.append(gradients[0].astype(jnp.bfloat16))
        state_list.append(gradients[1].astype(jnp.bfloat16))
        step_list.append(gradients[2])
        conv_value_total = conv_value_total + gradients[3]
        conv_state_total = conv_state_total + gradients[4]
        head_total = head_total + jnp.stack([gradients[5], gradients[6], gradients[7]])
    return (jnp.stack(mixed_list), jnp.stack(value_list), jnp.stack(state_list), jnp.stack(step_list), conv_value_total, conv_state_total, head_total)
```

```python
from functools import partial

import jax
import jax.numpy as jnp
from jax import lax
from jax.experimental import pallas as pl
from jax.experimental.pallas import tpu as pltpu
from jax.sharding import PartitionSpec as P

HEAD_DIM = 64
STATE = 128
KERNEL = 4
SUB = 128
PAIR = 2
LANES = PAIR * HEAD_DIM
LOG2E = 1.4426950408889634

precise = lax.Precision.HIGHEST
f32 = jnp.float32
bf16 = jnp.bfloat16


def shifted(value, axis, steps):
    count = lax.axis_size(axis)
    leading, last = (max(0, -steps), min(count, count - steps))
    return lax.ppermute(value, axis, [(source, source + steps) for source in range(leading, last)])


def token_starts(lengths, positions):
    doc_ends = jnp.cumsum(lengths)
    passed = doc_ends[None, :] <= positions[:, None]
    return jnp.sum(jnp.where(passed, lengths[None, :], 0), axis=1)


def causal_conv(series, weights, usable, rim_rows):
    padded = jnp.concatenate([rim_rows, series], axis=0)
    length = series.shape[0]
    summed = jnp.zeros(series.shape, f32)
    for offset in range(KERNEL):
        summed = summed + weights[offset][None, :] * padded[offset : offset + length] * usable[offset][:, None]
    return jax.nn.silu(summed)


def split(value):
    high = value.astype(bf16)
    return high, (value - high.astype(f32)).astype(bf16)


def mm(a, b):
    return jnp.dot(a, b, preferred_element_type=f32)


def mm_nt(a, b):
    return lax.dot_general(a, b, (((1,), (1,)), ((), ())), preferred_element_type=f32)


def mm3(a, b):
    (ah, al), (bh, bl) = a, b
    return mm(ah, bh) + (mm(al, bh) + mm(ah, bl))


def mm3_nt(a, b):
    (ah, al), (bh, bl) = a, b
    return mm_nt(ah, bh) + (mm_nt(al, bh) + mm_nt(ah, bl))


def first_lanes(rows):
    return lax.broadcasted_iota(jnp.int32, (rows, LANES), 1) < HEAD_DIM


def spread(columns, which):
    left = columns[:, PAIR * which : PAIR * which + 1]
    right = columns[:, PAIR * which + 1 : PAIR * which + 2]
    return jnp.where(first_lanes(columns.shape[0]), left, right)


C_CUM, C_STEP, C_NEAR, C_FAR, C_ENTER, C_LEAVE = range(6)


def sigmoid(value):
    return 1.0 / (1.0 + jnp.exp(-value))


def states_kernel(x, rim, dy, taps, usable, cols, write_t, read_t, pre_out, fresh, back, pad, wt_s, rt_s):
    rows = x.shape[0]

    @pl.when(pl.program_id(0) == 0)
    def _():
        wt_s[0], wt_s[1] = split(write_t[...])
        rt_s[0], rt_s[1] = split(read_t[...])

    pad[0:8] = rim[...]
    pad[8 : 8 + rows] = x[...].astype(f32)
    pre = jnp.zeros((rows, LANES), f32)
    for k in range(KERNEL):
        term = taps[k : k + 1, :] * pad[5 + k : 5 + k + rows]
        if k < KERNEL - 1:
            term = term * usable[:, k * LANES : (k + 1) * LANES]
        pre = pre + term
    pre_out[...] = pre
    columns = cols[0]
    weighted = pre * sigmoid(pre) * (spread(columns, C_STEP) * spread(columns, C_LEAVE))
    fresh[...] = mm3((wt_s[0], wt_s[1]), split(weighted))
    grad = dy[...].astype(f32) * spread(columns, C_ENTER)
    back[...] = mm3((rt_s[0], rt_s[1]), split(grad))


def local_kernel(pre_ref, dy, cols, rows_ref, gram, gram_t, y_out, u_out, dgram, g_s, gt_s):
    rows = dy.shape[0]
    blocks = rows // SUB
    half = rows // 2

    @pl.when(pl.program_id(0) == 0)
    def _():
        dgram[...] = jnp.zeros_like(dgram)
        g_s[0], g_s[1] = split(gram[...])
        gt_s[0], gt_s[1] = split(gram_t[...])

    columns = cols[0]
    lanes = first_lanes(SUB)
    zero = jnp.zeros((SUB, LANES), f32)
    pre = pre_ref[...]
    xs = pre * sigmoid(pre) * spread(columns, C_STEP)
    grad = dy[...].astype(f32)
    for b in range(blocks):
        at = slice(b * SUB, (b + 1) * SUB)
        decays, m, mt = [], [], []
        for j in range(PAIR):
            down = columns[at, j : j + 1]
            across = rows_ref[0, j : j + 1, at]
            gap = down - across
            decay = jnp.exp2(jnp.minimum(gap, 0.0))
            decays.append(decay)
            m.append(gram[at, at] * decay)
            mt.append(gram_t[at, at] * jnp.exp2(jnp.minimum(-gap, 0.0)))
        mh, ml = split(jnp.concatenate(m, axis=1))
        mth, mtl = split(jnp.concatenate(mt, axis=1))
        xb = xs[at]
        high = xb.astype(bf16).astype(f32)
        low = xb - high
        xbh = jnp.concatenate([jnp.where(lanes, high, zero), jnp.where(lanes, zero, high)], axis=0).astype(bf16)
        xbl = jnp.concatenate([jnp.where(lanes, low, zero), jnp.where(lanes, zero, low)], axis=0).astype(bf16)
        gb = grad[at]
        gbd = jnp.concatenate([jnp.where(lanes, gb, zero), jnp.where(lanes, zero, gb)], axis=0).astype(bf16)
        both = mm(mh, jnp.concatenate([xbh, xbl], axis=1))
        y_out[at] = both[:, :LANES] + (both[:, LANES:] + mm(ml, xbh))
        u_out[at] = mm(mth, gbd) + mm(mtl, gbd)
        d = mm_nt(
            jnp.concatenate([gbd, gbd], axis=1),
            jnp.concatenate([high.astype(bf16), low.astype(bf16)], axis=1),
        )
        dgram[at, at] += d[:SUB] * decays[0] + d[SUB:] * decays[1]

    def across_blocks(low, mid, top, which):
        early, late = slice(low, mid), slice(mid, top)
        factor = spread(columns[low:top], which)
        size = mid - low
        fe, fl = factor[:size], factor[size:]
        source = split(fe * xs[early])
        target = split(fl * grad[late])
        y_out[late] += fl * mm3((g_s[0, late, early], g_s[1, late, early]), source)
        u_out[early] += fe * mm3((gt_s[0, early, late], gt_s[1, early, late]), target)
        dgram[late, early] += mm3_nt(target, source)

    for b in range(0, blocks, 2):
        across_blocks(b * SUB, (b + 1) * SUB, (b + 2) * SUB, C_NEAR)
    across_blocks(0, half, rows, C_FAR)


def final_kernel(
    pre_ref, x, rim, dy, cols, usable, taps, skip, projected, entering, leaving, y_in, u_in,
    mixed, vgrad, tail, rim_out, tap_grad, token_sums, skip_sums, dproj,
    pad, dpad, p_s,
):
    rows = dy.shape[0]

    @pl.when(pl.program_id(0) == 0)
    def _():
        dproj[...] = jnp.zeros_like(dproj)
        p_s[0], p_s[1] = split(projected[...])
        dpad[0:8] = jnp.zeros((8, LANES), f32)
        dpad[8 + rows : 16 + rows] = jnp.zeros((8, LANES), f32)

    write = (p_s[0, :, :STATE], p_s[1, :, :STATE])
    read = (p_s[0, :, STATE:], p_s[1, :, STATE:])
    columns = cols[0]
    pre = pre_ref[...]
    gate = sigmoid(pre)
    values = pre * gate
    step = spread(columns, C_STEP)
    grad = dy[...].astype(f32)
    ent = split(entering[...])
    lea = split(leaving[...])
    enter = spread(columns, C_ENTER)
    leave = spread(columns, C_LEAVE)
    y = y_in[...] + enter * mm3(read, ent)
    u = u_in[...] + leave * mm3(write, lea)
    dproj[:, STATE:] += mm3_nt(split(enter * grad), ent)
    dproj[:, :STATE] += mm3_nt(split(leave * step * values), lea)
    gain = skip[0:1, :]
    mixed[...] = (y + gain * values).astype(bf16)
    dvalues = step * u + gain * grad
    skip_sums[0] = jnp.broadcast_to(jnp.sum(grad * values, axis=0, keepdims=True), (8, LANES))
    lane = lax.broadcasted_iota(jnp.int32, (8, LANES), 1) // HEAD_DIM
    row = lax.broadcasted_iota(jnp.int32, (8, LANES), 0)
    chosen = jnp.where(row == lane, 1.0, 0.0).astype(bf16)
    chosen = jnp.concatenate([chosen, chosen], axis=1)
    first = mm_nt(chosen, jnp.concatenate(split(grad * y), axis=1))
    second = mm_nt(chosen, jnp.concatenate(split(values * u), axis=1))
    token_sums[0, 0:2] = first[0:2]
    token_sums[0, 2:4] = second[0:2]
    dpre = dvalues * (gate * (1.0 + pre * (1.0 - gate)))

    pad[0:8] = rim[...]
    pad[8 : 8 + rows] = x[...].astype(f32)
    total = jnp.zeros((rows + 8, LANES), f32)
    for k in range(KERNEL):
        part = dpre
        if k < KERNEL - 1:
            part = part * usable[:, k * LANES : (k + 1) * LANES]
        tap_grad[k : k + 1, :] = jnp.sum(part * pad[5 + k : 5 + k + rows], axis=0, keepdims=True)
        dpad[8 : 8 + rows] = part
        total = total + taps[k : k + 1, :] * dpad[3 - k + 0 : 3 - k + rows + 8]
    rim_out[...] = total[0:8]
    vgrad[...] = total[8:].astype(bf16)
    tail[...] = total[rows:]


def on_device(
    value_input,
    state_proj,
    step_raw,
    doc_lengths,
    conv_value,
    conv_state,
    step_bias,
    decay_log,
    skip_gain,
    out_grad,
    interpret=False,
):
    rows, channels = value_input.shape[1:]
    heads = step_raw.shape[1]
    pairs = heads // PAIR
    blocks = rows // SUB
    half = rows // 2
    rim = KERNEL - 1
    ctx_place = lax.axis_index("ctx")
    context_count = lax.axis_size("ctx")
    whole = rows * context_count
    reach = min(context_count - 1, (whole // 2 - 2) // rows + 1)
    dev_start = ctx_place * rows
    positions = dev_start + jnp.arange(rows, dtype=jnp.int32)
    starts = token_starts(doc_lengths[0], positions)
    x = value_input[0]
    dy = out_grad[0]
    tail_rows = rows - rim
    rims = shifted(jnp.concatenate([x[tail_rows:], state_proj[0, tail_rows:]], axis=1), "ctx", 1)
    value_rim = jnp.concatenate([jnp.zeros((8 - rim, channels), f32), rims[:, :channels].astype(f32)], axis=0)
    state_rim = rims[:, channels:].astype(f32)

    usable = [(positions - rim + k >= starts).astype(f32) for k in range(KERNEL)]
    usable_wide = jnp.concatenate(
        [jnp.broadcast_to(usable[k][:, None], (rows, LANES)) for k in range(rim)], axis=1
    )
    projected, state_pullback = jax.vjp(
        lambda series, weights, rim_rows: causal_conv(series, weights, usable, rim_rows),
        state_proj[0].astype(f32), conv_state, state_rim,
    )
    write_rows, read_rows = projected[:, :STATE], projected[:, STATE:]
    allowed = (positions[None, :] <= positions[:, None]) & (positions[None, :] >= starts[:, None])
    gram = jnp.where(allowed, jnp.dot(read_rows, write_rows.T, precision=precise), 0.0)
    gram_t = jnp.where(allowed.T, jnp.dot(write_rows, read_rows.T, precision=precise), 0.0)

    logits = step_raw[0] + step_bias[:, None]
    step = jax.nn.softplus(logits)
    rate = jnp.exp(decay_log)[:, None]
    log_decay = -rate * step
    index = jnp.arange(SUB)
    upper = (index[:, None] <= index[None, :]).astype(f32)
    cum = jnp.einsum("hbs,st->hbt", log_decay.reshape(heads, blocks, SUB), upper, precision=precise)
    totals = cum[:, :, -1]

    def flat(value):
        return value.reshape(heads, rows)

    def before(first, block):
        return sum((totals[:, i] for i in range(first, block)), jnp.zeros((heads,), f32))

    near, far, enter, leave = [], [], [], []
    for b in range(blocks):
        inner = cum[:, b]
        rest = totals[:, b : b + 1] - inner
        near.append(inner if b % 2 else rest)
        if b >= blocks // 2:
            far.append(inner + before(blocks // 2, b)[:, None])
        else:
            far.append(rest + before(b + 1, blocks // 2)[:, None])
        enter.append(inner + before(0, b)[:, None])
        leave.append(rest + before(b + 1, blocks)[:, None])
    near, far, enter, leave = (jnp.exp(jnp.concatenate(v, axis=1)) for v in (near, far, enter, leave))
    enter = enter * (starts < dev_start).astype(f32)[None]
    leave = leave * (positions >= starts[-1]).astype(f32)[None]
    keep = jnp.exp(before(0, blocks)) * (starts[-1] < dev_start).astype(f32)
    cum2 = flat(cum) * LOG2E
    cols = jnp.stack([cum2, step, near, far, enter, leave])
    cols = cols.reshape(6, pairs, PAIR, rows).transpose(1, 3, 0, 2).reshape(pairs, rows, 6 * PAIR)
    row_form = cum2.reshape(pairs, PAIR, rows)

    col_spec = pl.BlockSpec((rows, LANES), lambda g: (0, g))
    cols_spec = pl.BlockSpec((1, rows, 6 * PAIR), lambda g: (g, 0, 0))
    eight_spec = pl.BlockSpec((8, LANES), lambda g: (0, g))
    taps_spec = pl.BlockSpec((KERNEL, LANES), lambda g: (0, g))
    state_spec = pl.BlockSpec((STATE, LANES), lambda g: (0, g))

    def fixed(*shape):
        return pl.BlockSpec(shape, lambda g: (0,) * len(shape))

    def like(*shape, dtype=f32):
        return jax.ShapeDtypeStruct(shape, dtype)

    params = pltpu.CompilerParams(
        dimension_semantics=("arbitrary",), vmem_limit_bytes=48 * 1024 * 1024
    )
    pre, fresh, back = pl.pallas_call(
        states_kernel,
        grid=(pairs,),
        in_specs=[col_spec, eight_spec, col_spec, taps_spec, fixed(rows, rim * LANES), cols_spec,
                  fixed(STATE, rows), fixed(STATE, rows)],
        out_specs=[col_spec, state_spec, state_spec],
        out_shape=[like(rows, channels), like(STATE, channels), like(STATE, channels)],
        scratch_shapes=[pltpu.VMEM((rows + 8, LANES), f32), pltpu.VMEM((2, STATE, rows), bf16),
                        pltpu.VMEM((2, STATE, rows), bf16)],
        compiler_params=params,
        interpret=interpret,
        name="states",
    )(x, value_rim, dy, conv_value, usable_wide, cols, write_rows.T, read_rows.T)

    keeps = lax.all_gather(keep, "ctx")

    def wide(value):
        return jnp.repeat(value, HEAD_DIM)[None, :]

    entering = jnp.zeros_like(fresh)
    leaving = jnp.zeros_like(back)
    ahead_keep = jnp.ones_like(keep)
    behind_keep = jnp.ones_like(keep)
    for j in range(1, reach + 1):
        entering = entering + wide(ahead_keep) * shifted(fresh, "ctx", j)
        leaving = leaving + wide(behind_keep) * shifted(back, "ctx", -j)
        ahead_keep = ahead_keep * keeps[jnp.clip(ctx_place - j, 0, context_count - 1)]
        behind_keep = behind_keep * keeps[jnp.clip(ctx_place + j, 0, context_count - 1)]

    y_local, u_local, dgram = pl.pallas_call(
        local_kernel,
        grid=(pairs,),
        in_specs=[col_spec, col_spec, cols_spec, pl.BlockSpec((1, PAIR, rows), lambda g: (g, 0, 0)),
                  fixed(rows, rows), fixed(rows, rows)],
        out_specs=[col_spec, col_spec, fixed(rows, rows)],
        out_shape=[like(rows, channels), like(rows, channels), like(rows, rows)],
        scratch_shapes=[pltpu.VMEM((2, rows, rows), bf16), pltpu.VMEM((2, rows, rows), bf16)],
        compiler_params=params,
        cost_estimate=pl.CostEstimate(flops=30 * 10**9, bytes_accessed=20 * 10**6, transcendentals=10**7),
        interpret=interpret,
        name="local",
    )(pre, dy, cols, row_form, gram, gram_t)

    mixed, vgrad, tail, rim_grad, tap_grad, token_sums, skip_sums, dproj = pl.pallas_call(
        final_kernel,
        grid=(pairs,),
        in_specs=[col_spec, col_spec, eight_spec, col_spec, cols_spec, fixed(rows, rim * LANES), taps_spec,
                  pl.BlockSpec((1, LANES), lambda g: (0, g)), fixed(rows, 2 * STATE), state_spec, state_spec,
                  col_spec, col_spec],
        out_specs=[col_spec, col_spec, eight_spec, eight_spec, taps_spec,
                   pl.BlockSpec((1, 2 * PAIR, rows), lambda g: (g, 0, 0)),
                   pl.BlockSpec((1, 8, LANES), lambda g: (g, 0, 0)), fixed(rows, 2 * STATE)],
        out_shape=[like(rows, channels, dtype=bf16), like(rows, channels, dtype=bf16), like(8, channels),
                   like(8, channels), like(KERNEL, channels), like(pairs, 2 * PAIR, rows),
                   like(pairs, 8, LANES), like(rows, 2 * STATE)],
        scratch_shapes=[pltpu.VMEM((rows + 8, LANES), f32), pltpu.VMEM((rows + 16, LANES), f32),
                        pltpu.VMEM((2, rows, 2 * STATE), bf16)],
        compiler_params=params,
        interpret=interpret,
        name="final",
    )(pre, x, value_rim, dy, cols, usable_wide, conv_value, wide(skip_gain), projected, entering, leaving,
      y_local, u_local)

    dgram = jnp.where(allowed, dgram, 0.0)
    dread = jnp.dot(dgram, write_rows, precision=precise)
    dwrite = jnp.dot(dgram.T, read_rows, precision=precise)
    dprojected = dproj + jnp.concatenate([dwrite, dread], axis=1)
    dstate, dconv_state, dstate_rim = state_pullback(dprojected)

    sums = token_sums.reshape(pairs, 2, PAIR, rows)
    out_dot = sums[:, 0].reshape(heads, rows)
    in_dot = sums[:, 1].reshape(heads, rows)
    closing = jnp.sum(leaving * (wide(keep) * entering + fresh), axis=0)
    closing = jnp.sum(closing.reshape(heads, HEAD_DIM), axis=1)
    dcum = out_dot - step * in_dot
    order = jnp.arange(rows)
    later = (order[:, None] >= order[None, :]).astype(f32)
    dlog = jnp.dot(dcum, later, precision=precise) + closing[:, None]
    dstep = in_dot - rate * dlog
    step_grad = dstep * jax.nn.sigmoid(logits)
    head_part = jnp.stack([
        jnp.sum(step_grad, axis=1),
        jnp.sum(dlog * log_decay, axis=1),
        jnp.sum(skip_sums[:, 0].reshape(heads, HEAD_DIM), axis=1),
    ])

    rims_back = shifted(jnp.concatenate([rim_grad[8 - rim :], dstate_rim], axis=1), "ctx", -1)
    tail_total = tail.at[8 - rim :].add(rims_back[:, :channels])
    value_grad = lax.dynamic_update_slice(vgrad, tail_total.astype(bf16), (rows - 8, 0))
    state_partial = dstate.at[tail_rows:].add(rims_back[:, channels:])
    state_grad = lax.psum(state_partial, "head").astype(bf16)
    conv_value_grad, head_grads = lax.psum((tap_grad, head_part), ("dp", "ctx"))
    conv_state_grad = lax.psum(dconv_state, ("dp", "ctx", "head"))
    return (
        mixed[None],
        value_grad[None],
        state_grad[None],
        step_grad[None],
        conv_value_grad,
        conv_state_grad,
        head_grads,
    )


def solution(mesh, interpret=False):
    return jax.shard_map(
        partial(on_device, interpret=interpret),
        mesh=mesh,
        in_specs=(
            P("dp", "ctx", "head"),
            P("dp", "ctx", None),
            P("dp", "head", "ctx"),
            P("dp", None),
            P(None, "head"),
            P(),
            P("head"),
            P("head"),
            P("head"),
            P("dp", "ctx", "head"),
        ),
        out_specs=(
            P("dp", "ctx", "head"),
            P("dp", "ctx", "head"),
            P("dp", "ctx", None),
            P("dp", "head", "ctx"),
            P(None, "head"),
            P(),
            P(None, "head"),
        ),
        check_vma=False,
    )
```

```python
from functools import partial

import jax
import jax.numpy as jnp
from jax import lax
from jax.experimental import pallas as pl
from jax.experimental.pallas import tpu as pltpu
from jax.sharding import PartitionSpec as P

HEAD_DIM = 64
STATE = 128
KERNEL = 4
SUB = 128
PAIR = 2
LANES = PAIR * HEAD_DIM
LOG2E = 1.4426950408889634

precise = lax.Precision.HIGHEST
f32 = jnp.float32
bf16 = jnp.bfloat16


def shifted(value, axis, steps):
    count = lax.axis_size(axis)
    leading, last = (max(0, -steps), min(count, count - steps))
    return lax.ppermute(value, axis, [(source, source + steps) for source in range(leading, last)])


def token_starts(lengths, positions):
    doc_ends = jnp.cumsum(lengths)
    passed = doc_ends[None, :] <= positions[:, None]
    return jnp.sum(jnp.where(passed, lengths[None, :], 0), axis=1)


def causal_conv(series, weights, usable, rim_rows):
    padded = jnp.concatenate([rim_rows, series], axis=0)
    length = series.shape[0]
    summed = jnp.zeros(series.shape, f32)
    for offset in range(KERNEL):
        summed = summed + weights[offset][None, :] * padded[offset : offset + length] * usable[offset][:, None]
    return jax.nn.silu(summed)


def split(value):
    high = value.astype(bf16)
    return high, (value - high.astype(f32)).astype(bf16)


def mm(a, b):
    return jnp.dot(a, b, preferred_element_type=f32)


def mm_nt(a, b):
    return lax.dot_general(a, b, (((1,), (1,)), ((), ())), preferred_element_type=f32)


def mm3(a, b):
    (ah, al), (bh, bl) = a, b
    return mm(ah, bh) + (mm(al, bh) + mm(ah, bl))


def mm3_nt(a, b):
    (ah, al), (bh, bl) = a, b
    return mm_nt(ah, bh) + (mm_nt(al, bh) + mm_nt(ah, bl))


def first_lanes(rows):
    return lax.broadcasted_iota(jnp.int32, (rows, LANES), 1) < HEAD_DIM


def spread(columns, which):
    left = columns[:, PAIR * which : PAIR * which + 1]
    right = columns[:, PAIR * which + 1 : PAIR * which + 2]
    return jnp.where(first_lanes(columns.shape[0]), left, right)


C_CUM, C_STEP, C_NEAR, C_FAR, C_ENTER, C_LEAVE = range(6)


def sigmoid(value):
    return 1.0 / (1.0 + jnp.exp(-value))


def states_kernel(x, rim, dy, taps, usable, cols, write_t, read_t, keep, pre_out, fresh, back, pad, wt_s, rt_s):
    rows = x.shape[0]

    @pl.when(pl.program_id(0) == 0)
    def _():
        wt_s[0], wt_s[1] = split(write_t[...])
        rt_s[0], rt_s[1] = split(read_t[...])

    pad[0:8] = rim[...]
    pad[8 : 8 + rows] = x[...].astype(f32)
    pre = jnp.zeros((rows, LANES), f32)
    for k in range(KERNEL):
        term = taps[k : k + 1, :] * pad[5 + k : 5 + k + rows]
        if k < KERNEL - 1:
            term = term * usable[:, k * LANES : (k + 1) * LANES]
        pre = pre + term
    pre_out[...] = pre
    columns = cols[0]
    weighted = pre * sigmoid(pre) * (spread(columns, C_STEP) * spread(columns, C_LEAVE))
    fresh[:STATE] = mm3((wt_s[0], wt_s[1]), split(weighted))
    fresh[STATE:] = jnp.broadcast_to(keep[...], (8, LANES))
    grad = dy[...].astype(f32) * spread(columns, C_ENTER)
    back[:STATE] = mm3((rt_s[0], rt_s[1]), split(grad))
    back[STATE:] = jnp.broadcast_to(keep[...], (8, LANES))


def local_kernel(pre_ref, dy, cols, rows_ref, gram, gram_t, y_out, u_out, dgram, g_s, gt_s):
    rows = dy.shape[0]
    blocks = rows // SUB
    half = rows // 2

    @pl.when(pl.program_id(0) == 0)
    def _():
        dgram[...] = jnp.zeros_like(dgram)
        g_s[0], g_s[1] = split(gram[...])
        gt_s[0], gt_s[1] = split(gram_t[...])

    columns = cols[0]
    lanes = first_lanes(SUB)
    zero = jnp.zeros((SUB, LANES), f32)
    pre = pre_ref[...]
    xs = pre * sigmoid(pre) * spread(columns, C_STEP)
    grad = dy[...].astype(f32)
    for b in range(blocks):
        at = slice(b * SUB, (b + 1) * SUB)
        decays, m, mt = [], [], []
        for j in range(PAIR):
            down = columns[at, j : j + 1]
            across = rows_ref[0, j : j + 1, at]
            gap = down - across
            decay = jnp.exp2(jnp.minimum(gap, 0.0))
            decays.append(decay)
            m.append(gram[at, at] * decay)
            mt.append(gram_t[at, at] * jnp.exp2(jnp.minimum(-gap, 0.0)))
        mh, ml = split(jnp.concatenate(m, axis=1))
        mth, mtl = split(jnp.concatenate(mt, axis=1))
        xb = xs[at]
        high = xb.astype(bf16).astype(f32)
        low = xb - high
        xbh = jnp.concatenate([jnp.where(lanes, high, zero), jnp.where(lanes, zero, high)], axis=0).astype(bf16)
        xbl = jnp.concatenate([jnp.where(lanes, low, zero), jnp.where(lanes, zero, low)], axis=0).astype(bf16)
        gb = grad[at]
        gbd = jnp.concatenate([jnp.where(lanes, gb, zero), jnp.where(lanes, zero, gb)], axis=0).astype(bf16)
        both = mm(mh, jnp.concatenate([xbh, xbl], axis=1))
        y_out[at] = both[:, :LANES] + (both[:, LANES:] + mm(ml, xbh))
        u_out[at] = mm(mth, gbd) + mm(mtl, gbd)
        d = mm_nt(
            jnp.concatenate([gbd, gbd], axis=1),
            jnp.concatenate([high.astype(bf16), low.astype(bf16)], axis=1),
        )
        dgram[at, at] += d[:SUB] * decays[0] + d[SUB:] * decays[1]

    def across_blocks(low, mid, top, which):
        early, late = slice(low, mid), slice(mid, top)
        factor = spread(columns[low:top], which)
        size = mid - low
        fe, fl = factor[:size], factor[size:]
        source = split(fe * xs[early])
        target = split(fl * grad[late])
        y_out[late] += fl * mm3((g_s[0, late, early], g_s[1, late, early]), source)
        u_out[early] += fe * mm3((gt_s[0, early, late], gt_s[1, early, late]), target)
        dgram[late, early] += mm3_nt(target, source)

    for b in range(0, blocks, 2):
        across_blocks(b * SUB, (b + 1) * SUB, (b + 2) * SUB, C_NEAR)
    across_blocks(0, half, rows, C_FAR)


def final_kernel(
    pre_ref, x, rim, dy, cols, usable, taps, skip, projected, entering, leaving, y_in, u_in,
    mixed, vgrad, tail, rim_out, tap_grad, token_sums, skip_sums, dproj,
    pad, dpad, p_s,
):
    rows = dy.shape[0]

    @pl.when(pl.program_id(0) == 0)
    def _():
        dproj[...] = jnp.zeros_like(dproj)
        p_s[0], p_s[1] = split(projected[...])
        dpad[0:8] = jnp.zeros((8, LANES), f32)
        dpad[8 + rows : 16 + rows] = jnp.zeros((8, LANES), f32)

    write = (p_s[0, :, :STATE], p_s[1, :, :STATE])
    read = (p_s[0, :, STATE:], p_s[1, :, STATE:])
    columns = cols[0]
    pre = pre_ref[...]
    gate = sigmoid(pre)
    values = pre * gate
    step = spread(columns, C_STEP)
    grad = dy[...].astype(f32)
    ent = split(entering[...])
    lea = split(leaving[...])
    enter = spread(columns, C_ENTER)
    leave = spread(columns, C_LEAVE)
    y = y_in[...] + enter * mm3(read, ent)
    u = u_in[...] + leave * mm3(write, lea)
    dproj[:, STATE:] += mm3_nt(split(enter * grad), ent)
    dproj[:, :STATE] += mm3_nt(split(leave * step * values), lea)
    gain = skip[0:1, :]
    mixed[...] = (y + gain * values).astype(bf16)
    dvalues = step * u + gain * grad
    skip_sums[0] = jnp.broadcast_to(jnp.sum(grad * values, axis=0, keepdims=True), (8, LANES))
    lane = lax.broadcasted_iota(jnp.int32, (8, LANES), 1) // HEAD_DIM
    row = lax.broadcasted_iota(jnp.int32, (8, LANES), 0)
    chosen = jnp.where(row == lane, 1.0, 0.0).astype(bf16)
    chosen = jnp.concatenate([chosen, chosen], axis=1)
    first = mm_nt(chosen, jnp.concatenate(split(grad * y), axis=1))
    second = mm_nt(chosen, jnp.concatenate(split(values * u), axis=1))
    token_sums[0, 0:2] = first[0:2]
    token_sums[0, 2:4] = second[0:2]
    dpre = dvalues * (gate * (1.0 + pre * (1.0 - gate)))

    pad[0:8] = rim[...]
    pad[8 : 8 + rows] = x[...].astype(f32)
    total = jnp.zeros((rows + 8, LANES), f32)
    for k in range(KERNEL):
        part = dpre
        if k < KERNEL - 1:
            part = part * usable[:, k * LANES : (k + 1) * LANES]
        tap_grad[k : k + 1, :] = jnp.sum(part * pad[5 + k : 5 + k + rows], axis=0, keepdims=True)
        dpad[8 : 8 + rows] = part
        total = total + taps[k : k + 1, :] * dpad[3 - k + 0 : 3 - k + rows + 8]
    rim_out[...] = total[0:8]
    vgrad[...] = total[8:].astype(bf16)
    tail[...] = total[rows:]


def sum_kernel(
    groups, members, local_rows, part, small, state_out, small_out, cs_out,
    part_in, small_in, chunk, chunk_in, cs_in, send_p, recv_p, send_s, recv_s, send_c, recv_c, send_k, recv_k,
):
    ctx = lax.axis_size("ctx")
    me = lax.axis_index("head")
    mine = lax.axis_index("dp") * ctx + lax.axis_index("ctx")
    size = part.shape[0] // groups

    def along(offset):
        return {"head": lax.rem(me + offset, groups)}

    def beside(offset):
        other = lax.rem(mine + offset, members)
        return {"dp": other // ctx, "ctx": lax.rem(other, ctx)}

    def remote(src, dst, send, recv, device):
        return pltpu.make_async_remote_copy(
            src_ref=src, dst_ref=dst, send_sem=send, recv_sem=recv, device_id=device,
            device_id_type=pl.DeviceIdType.MESH,
        )

    barrier = pltpu.get_barrier_semaphore()
    for o in range(1, groups):
        pl.semaphore_signal(barrier, inc=1, device_id=along(o), device_id_type=pl.DeviceIdType.MESH)
    for o in range(1, members):
        pl.semaphore_signal(barrier, inc=1, device_id=beside(o), device_id_type=pl.DeviceIdType.MESH)
    pl.semaphore_wait(barrier, groups + members - 2)

    first = []
    for o in range(1, groups):
        to = lax.rem(me + o, groups)
        src = part.at[pl.ds(pl.multiple_of(to * size, size), size)]
        first.append(remote(src, part_in.at[o - 1], send_p.at[o - 1], recv_p.at[o - 1], along(o)))
    for o in range(1, members):
        first.append(remote(small, small_in.at[o - 1], send_s.at[o - 1], recv_s.at[o - 1], beside(o)))
    for copy in first:
        copy.start()
    for copy in first:
        copy.wait()

    total = part[pl.ds(pl.multiple_of(me * size, size), size), :]
    for o in range(1, groups):
        total = total + part_in[o - 1]
    chunk[...] = total.astype(bf16)

    def in_order(own, slots, place, count):
        result = None
        for s in range(count):
            slot = jnp.maximum(lax.rem(place - s + count, count) - 1, 0)
            term = jnp.where(place == s, own, slots[slot])
            result = term if result is None else result + term
        return result

    summed = in_order(small[...], small_in, mine, members)
    small_out[...] = summed[:local_rows]
    cs_out[...] = summed[local_rows:]
    second = []
    for o in range(1, groups):
        second.append(remote(chunk, chunk_in.at[o - 1], send_c.at[o - 1], recv_c.at[o - 1], along(o)))
        second.append(remote(cs_out, cs_in.at[o - 1], send_k.at[o - 1], recv_k.at[o - 1], along(o)))
    for copy in second:
        copy.start()
    state_out[pl.ds(pl.multiple_of(me * size, size), size), :] = chunk[...]
    for copy in second:
        copy.wait()
    for o in range(1, groups):
        origin = lax.rem(me - o + groups, groups)
        state_out[pl.ds(pl.multiple_of(origin * size, size), size), :] = chunk_in[o - 1]
    cs_out[...] = in_order(cs_out[...], cs_in, me, groups)


def sum_across(part, small, local_rows):
    groups = lax.axis_size("head")
    members = lax.axis_size("dp") * lax.axis_size("ctx")
    rows, width = part.shape
    extra = small.shape[0] - local_rows
    size = rows // groups
    vmem = pl.BlockSpec(memory_space=pltpu.VMEM)
    dma = pltpu.SemaphoreType.DMA
    return pl.pallas_call(
        partial(sum_kernel, groups, members, local_rows),
        in_specs=[vmem, vmem],
        out_specs=[vmem, vmem, vmem],
        out_shape=[jax.ShapeDtypeStruct((rows, width), bf16), jax.ShapeDtypeStruct((local_rows, 128), f32),
                   jax.ShapeDtypeStruct((extra, 128), f32)],
        scratch_shapes=[
            pltpu.VMEM((groups - 1, size, width), f32),
            pltpu.VMEM((members - 1, *small.shape), f32),
            pltpu.VMEM((size, width), bf16),
            pltpu.VMEM((groups - 1, size, width), bf16),
            pltpu.VMEM((groups - 1, extra, 128), f32),
            dma((groups - 1,)), dma((groups - 1,)), dma((members - 1,)), dma((members - 1,)),
            dma((groups - 1,)), dma((groups - 1,)), dma((groups - 1,)), dma((groups - 1,)),
        ],
        compiler_params=pltpu.CompilerParams(
            collective_id=0, has_side_effects=True, vmem_limit_bytes=32 * 1024 * 1024
        ),
        name="sums",
    )(part, small)


def on_device(
    value_input,
    state_proj,
    step_raw,
    doc_lengths,
    conv_value,
    conv_state,
    step_bias,
    decay_log,
    skip_gain,
    out_grad,
    interpret=False,
):
    rows, channels = value_input.shape[1:]
    heads = step_raw.shape[1]
    pairs = heads // PAIR
    blocks = rows // SUB
    half = rows // 2
    rim = KERNEL - 1
    ctx_place = lax.axis_index("ctx")
    context_count = lax.axis_size("ctx")
    whole = rows * context_count
    reach = min(context_count - 1, (whole // 2 - 2) // rows + 1)
    dev_start = ctx_place * rows
    positions = dev_start + jnp.arange(rows, dtype=jnp.int32)
    starts = token_starts(doc_lengths[0], positions)
    x = value_input[0]
    dy = out_grad[0]
    tail_rows = rows - rim
    rims = shifted(jnp.concatenate([x[tail_rows:], state_proj[0, tail_rows:]], axis=1), "ctx", 1)
    value_rim = jnp.concatenate([jnp.zeros((8 - rim, channels), f32), rims[:, :channels].astype(f32)], axis=0)
    state_rim = rims[:, channels:].astype(f32)

    usable = [(positions - rim + k >= starts).astype(f32) for k in range(KERNEL)]
    usable_wide = jnp.concatenate(
        [jnp.broadcast_to(usable[k][:, None], (rows, LANES)) for k in range(rim)], axis=1
    )
    projected, state_pullback = jax.vjp(
        lambda series, weights, rim_rows: causal_conv(series, weights, usable, rim_rows),
        state_proj[0].astype(f32), conv_state, state_rim,
    )
    write_rows, read_rows = projected[:, :STATE], projected[:, STATE:]
    allowed = (positions[None, :] <= positions[:, None]) & (positions[None, :] >= starts[:, None])
    gram = jnp.where(allowed, jnp.dot(read_rows, write_rows.T, precision=precise), 0.0)
    gram_t = jnp.where(allowed.T, jnp.dot(write_rows, read_rows.T, precision=precise), 0.0)

    logits = step_raw[0] + step_bias[:, None]
    step = jax.nn.softplus(logits)
    rate = jnp.exp(decay_log)[:, None]
    log_decay = -rate * step
    index = jnp.arange(SUB)
    upper = (index[:, None] <= index[None, :]).astype(f32)
    cum = jnp.einsum("hbs,st->hbt", log_decay.reshape(heads, blocks, SUB), upper, precision=precise)
    totals = cum[:, :, -1]

    def flat(value):
        return value.reshape(heads, rows)

    def before(first, block):
        return sum((totals[:, i] for i in range(first, block)), jnp.zeros((heads,), f32))

    near, far, enter, leave = [], [], [], []
    for b in range(blocks):
        inner = cum[:, b]
        rest = totals[:, b : b + 1] - inner
        near.append(inner if b % 2 else rest)
        if b >= blocks // 2:
            far.append(inner + before(blocks // 2, b)[:, None])
        else:
            far.append(rest + before(b + 1, blocks // 2)[:, None])
        enter.append(inner + before(0, b)[:, None])
        leave.append(rest + before(b + 1, blocks)[:, None])
    near, far, enter, leave = (jnp.exp(jnp.concatenate(v, axis=1)) for v in (near, far, enter, leave))
    enter = enter * (starts < dev_start).astype(f32)[None]
    leave = leave * (positions >= starts[-1]).astype(f32)[None]
    keep = jnp.exp(before(0, blocks)) * (starts[-1] < dev_start).astype(f32)
    cum2 = flat(cum) * LOG2E
    cols = jnp.stack([cum2, step, near, far, enter, leave])
    cols = cols.reshape(6, pairs, PAIR, rows).transpose(1, 3, 0, 2).reshape(pairs, rows, 6 * PAIR)
    row_form = cum2.reshape(pairs, PAIR, rows)

    col_spec = pl.BlockSpec((rows, LANES), lambda g: (0, g))
    cols_spec = pl.BlockSpec((1, rows, 6 * PAIR), lambda g: (g, 0, 0))
    eight_spec = pl.BlockSpec((8, LANES), lambda g: (0, g))
    taps_spec = pl.BlockSpec((KERNEL, LANES), lambda g: (0, g))
    one_spec = pl.BlockSpec((1, LANES), lambda g: (0, g))
    sent_spec = pl.BlockSpec((STATE + 8, LANES), lambda g: (0, g))
    state_spec = pl.BlockSpec((STATE, LANES), lambda g: (0, g))

    def wide(value):
        return jnp.repeat(value, HEAD_DIM)[None, :]

    def fixed(*shape):
        return pl.BlockSpec(shape, lambda g: (0,) * len(shape))

    def like(*shape, dtype=f32):
        return jax.ShapeDtypeStruct(shape, dtype)

    params = pltpu.CompilerParams(
        dimension_semantics=("arbitrary",), vmem_limit_bytes=48 * 1024 * 1024
    )
    pre, fresh, back = pl.pallas_call(
        states_kernel,
        grid=(pairs,),
        in_specs=[col_spec, eight_spec, col_spec, taps_spec, fixed(rows, rim * LANES), cols_spec,
                  fixed(STATE, rows), fixed(STATE, rows), one_spec],
        out_specs=[col_spec, sent_spec, sent_spec],
        out_shape=[like(rows, channels), like(STATE + 8, channels), like(STATE + 8, channels)],
        scratch_shapes=[pltpu.VMEM((rows + 8, LANES), f32), pltpu.VMEM((2, STATE, rows), bf16),
                        pltpu.VMEM((2, STATE, rows), bf16)],
        compiler_params=params,
        interpret=interpret,
        name="states",
    )(x, value_rim, dy, conv_value, usable_wide, cols, write_rows.T, read_rows.T, wide(keep))

    entering, leaving = jnp.zeros((2, STATE, channels), f32)
    ahead_keep, behind_keep = jnp.ones((2, 1, channels), f32)
    for j in range(1, reach + 1):
        ahead, behind = shifted(fresh, "ctx", j), shifted(back, "ctx", -j)
        entering = entering + ahead_keep * ahead[:STATE]
        leaving = leaving + behind_keep * behind[:STATE]
        ahead_keep = ahead_keep * ahead[STATE : STATE + 1]
        behind_keep = behind_keep * behind[STATE : STATE + 1]

    y_local, u_local, dgram = pl.pallas_call(
        local_kernel,
        grid=(pairs,),
        in_specs=[col_spec, col_spec, cols_spec, pl.BlockSpec((1, PAIR, rows), lambda g: (g, 0, 0)),
                  fixed(rows, rows), fixed(rows, rows)],
        out_specs=[col_spec, col_spec, fixed(rows, rows)],
        out_shape=[like(rows, channels), like(rows, channels), like(rows, rows)],
        scratch_shapes=[pltpu.VMEM((2, rows, rows), bf16), pltpu.VMEM((2, rows, rows), bf16)],
        compiler_params=params,
        cost_estimate=pl.CostEstimate(flops=30 * 10**9, bytes_accessed=20 * 10**6, transcendentals=10**7),
        interpret=interpret,
        name="local",
    )(pre, dy, cols, row_form, gram, gram_t)

    mixed, vgrad, tail, rim_grad, tap_grad, token_sums, skip_sums, dproj = pl.pallas_call(
        final_kernel,
        grid=(pairs,),
        in_specs=[col_spec, col_spec, eight_spec, col_spec, cols_spec, fixed(rows, rim * LANES), taps_spec,
                  pl.BlockSpec((1, LANES), lambda g: (0, g)), fixed(rows, 2 * STATE), state_spec, state_spec,
                  col_spec, col_spec],
        out_specs=[col_spec, col_spec, eight_spec, eight_spec, taps_spec,
                   pl.BlockSpec((1, 2 * PAIR, rows), lambda g: (g, 0, 0)),
                   pl.BlockSpec((1, 8, LANES), lambda g: (g, 0, 0)), fixed(rows, 2 * STATE)],
        out_shape=[like(rows, channels, dtype=bf16), like(rows, channels, dtype=bf16), like(8, channels),
                   like(8, channels), like(KERNEL, channels), like(pairs, 2 * PAIR, rows),
                   like(pairs, 8, LANES), like(rows, 2 * STATE)],
        scratch_shapes=[pltpu.VMEM((rows + 8, LANES), f32), pltpu.VMEM((rows + 16, LANES), f32),
                        pltpu.VMEM((2, rows, 2 * STATE), bf16)],
        compiler_params=params,
        interpret=interpret,
        name="final",
    )(pre, x, value_rim, dy, cols, usable_wide, conv_value, wide(skip_gain), projected, entering, leaving,
      y_local, u_local)

    dgram = jnp.where(allowed, dgram, 0.0)
    dread = jnp.dot(dgram, write_rows, precision=precise)
    dwrite = jnp.dot(dgram.T, read_rows, precision=precise)
    dprojected = dproj + jnp.concatenate([dwrite, dread], axis=1)
    dstate, dconv_state, dstate_rim = state_pullback(dprojected)

    sums = token_sums.reshape(pairs, 2, PAIR, rows)
    out_dot = sums[:, 0].reshape(heads, rows)
    in_dot = sums[:, 1].reshape(heads, rows)
    closing = jnp.sum(leaving * (wide(keep) * entering + fresh[:STATE]), axis=0)
    closing = jnp.sum(closing.reshape(heads, HEAD_DIM), axis=1)
    dcum = out_dot - step * in_dot
    order = jnp.arange(rows)
    later = (order[:, None] >= order[None, :]).astype(f32)
    dlog = jnp.dot(dcum, later, precision=precise) + closing[:, None]
    dstep = in_dot - rate * dlog
    step_grad = dstep * jax.nn.sigmoid(logits)
    head_part = jnp.stack([
        jnp.sum(step_grad, axis=1),
        jnp.sum(dlog * log_decay, axis=1),
        jnp.sum(skip_sums[:, 0].reshape(heads, HEAD_DIM), axis=1),
    ])

    rims_back = shifted(jnp.concatenate([rim_grad[8 - rim :], dstate_rim], axis=1), "ctx", -1)
    tail_total = tail.at[8 - rim :].add(rims_back[:, :channels])
    value_grad = lax.dynamic_update_slice(vgrad, tail_total.astype(bf16), (rows - 8, 0))
    state_partial = dstate.at[tail_rows:].add(rims_back[:, channels:])
    tap_rows = KERNEL * channels // 128
    head_flat = jnp.pad(head_part.reshape(-1), (0, 8 * 128 - 3 * heads)).reshape(8, 128)
    small = jnp.concatenate([tap_grad.reshape(tap_rows, 128), head_flat, dconv_state.reshape(-1, 128)])
    state_grad, small_sum, conv_state_sum = sum_across(state_partial, small, tap_rows + 8)
    conv_value_grad = small_sum[:tap_rows].reshape(KERNEL, channels)
    head_grads = small_sum[tap_rows:].reshape(-1)[: 3 * heads].reshape(3, heads)
    conv_state_grad = conv_state_sum.reshape(KERNEL, 2 * STATE)
    return (
        mixed[None],
        value_grad[None],
        state_grad[None],
        step_grad[None],
        conv_value_grad,
        conv_state_grad,
        head_grads,
    )


def solution(mesh, interpret=False):
    return jax.shard_map(
        partial(on_device, interpret=interpret),
        mesh=mesh,
        in_specs=(
            P("dp", "ctx", "head"),
            P("dp", "ctx", None),
            P("dp", "head", "ctx"),
            P("dp", None),
            P(None, "head"),
            P(),
            P("head"),
            P("head"),
            P("head"),
            P("dp", "ctx", "head"),
        ),
        out_specs=(
            P("dp", "ctx", "head"),
            P("dp", "ctx", "head"),
            P("dp", "ctx", None),
            P("dp", "head", "ctx"),
            P(None, "head"),
            P(),
            P(None, "head"),
        ),
        check_vma=False,
    )
```

```python
from functools import partial

import jax
import jax.numpy as jnp
from jax import lax
from jax.experimental import pallas as pl
from jax.experimental.pallas import tpu as pltpu
from jax.sharding import PartitionSpec as P

HEAD_DIM = 64
STATE = 128
KERNEL = 4
SUB = 128
PAIR = 2
LANES = PAIR * HEAD_DIM
LOG2E = 1.4426950408889634

precise = lax.Precision.HIGHEST
f32 = jnp.float32
bf16 = jnp.bfloat16


def shifted(value, axis, steps):
    count = lax.axis_size(axis)
    leading, last = (max(0, -steps), min(count, count - steps))
    return lax.ppermute(value, axis, [(source, source + steps) for source in range(leading, last)])


def token_starts(lengths, positions):
    doc_ends = jnp.cumsum(lengths)
    passed = doc_ends[None, :] <= positions[:, None]
    return jnp.sum(jnp.where(passed, lengths[None, :], 0), axis=1)


def causal_conv(series, weights, usable, rim_rows):
    padded = jnp.concatenate([rim_rows, series], axis=0)
    length = series.shape[0]
    summed = jnp.zeros(series.shape, f32)
    for offset in range(KERNEL):
        summed = summed + weights[offset][None, :] * padded[offset : offset + length] * usable[offset][:, None]
    return jax.nn.silu(summed)


def split(value):
    high = value.astype(bf16)
    return high, (value - high.astype(f32)).astype(bf16)


def mm(a, b):
    return jnp.dot(a, b, preferred_element_type=f32)


def mm_nt(a, b):
    return lax.dot_general(a, b, (((1,), (1,)), ((), ())), preferred_element_type=f32)


def mm3(a, b):
    (ah, al), (bh, bl) = a, b
    return mm(ah, bh) + (mm(al, bh) + mm(ah, bl))


def mm3_nt(a, b):
    (ah, al), (bh, bl) = a, b
    return mm_nt(ah, bh) + (mm_nt(al, bh) + mm_nt(ah, bl))


def first_lanes(rows):
    return lax.broadcasted_iota(jnp.int32, (rows, LANES), 1) < HEAD_DIM


def spread(columns, which):
    left = columns[:, PAIR * which : PAIR * which + 1]
    right = columns[:, PAIR * which + 1 : PAIR * which + 2]
    return jnp.where(first_lanes(columns.shape[0]), left, right)


C_CUM, C_STEP, C_NEAR, C_FAR, C_ENTER, C_LEAVE = range(6)


def sigmoid(value):
    return 1.0 / (1.0 + jnp.exp(-value))


def start_kernel(
    reach, x, rim, dy, taps, usable, cols, projected, keep, rows_ref, gram, gram_t,
    pre_out, y_out, u_out, dgram, entering, leaving, closing,
    pad, wt_s, rt_s, g_s, gt_s, xs_s, fresh, back, got, send_sem, recv_sem,
):
    phase, g = pl.program_id(0), pl.program_id(1)
    pairs = pl.num_programs(1)
    ctx, count = lax.axis_index("ctx"), lax.axis_size("ctx")
    rows = x.shape[0]

    def each_copy(pair, act_sent, act_got):
        for j in range(1, reach + 1):
            for way, (source, step) in enumerate(((fresh, j), (back, -j))):
                to, origin = ctx + step, ctx - step
                copy = pltpu.make_async_remote_copy(
                    src_ref=source.at[pair],
                    dst_ref=got.at[way, j - 1, pair],
                    send_sem=send_sem.at[way, j - 1, pair],
                    recv_sem=recv_sem.at[way, j - 1, pair],
                    device_id={"ctx": to},
                    device_id_type=pl.DeviceIdType.MESH,
                )
                pl.when((to >= 0) & (to < count))(partial(act_sent, copy))
                pl.when((origin >= 0) & (origin < count))(partial(act_got, copy))

    @pl.when((phase == 0) & (g == 0))
    def _():
        barrier = pltpu.get_barrier_semaphore()
        for o in range(1, count):
            pl.semaphore_signal(
                barrier, inc=1, device_id={"ctx": lax.rem(ctx + o, count)}, device_id_type=pl.DeviceIdType.MESH
            )
        pl.semaphore_wait(barrier, count - 1)

        for j in range(1, reach + 1):
            for way, origin in enumerate((ctx - j, ctx + j)):

                @pl.when((origin < 0) | (origin >= count))
                def _():
                    got[way, j - 1] = jnp.zeros(got.shape[2:], f32)

        wt_s[0], wt_s[1] = split(projected[:, :STATE].T)
        rt_s[0], rt_s[1] = split(projected[:, STATE:].T)

    @pl.when(phase == 0)
    def _():
        pad[0:8] = rim[...]
        pad[8 : 8 + rows] = x[...].astype(f32)
        pre = jnp.zeros((rows, LANES), f32)
        for k in range(KERNEL):
            term = taps[k : k + 1, :] * pad[5 + k : 5 + k + rows]
            if k < KERNEL - 1:
                term = term * usable[:, k * LANES : (k + 1) * LANES]
            pre = pre + term
        pre_out[...] = pre
        columns = cols[0]
        xs = pre * sigmoid(pre) * spread(columns, C_STEP)
        xs_s[g] = xs
        fresh[g, :STATE] = mm3((wt_s[0], wt_s[1]), split(xs * spread(columns, C_LEAVE)))
        fresh[g, STATE:] = jnp.broadcast_to(keep[...], (8, LANES))
        grad = dy[...].astype(f32) * spread(columns, C_ENTER)
        back[g, :STATE] = mm3((rt_s[0], rt_s[1]), split(grad))
        back[g, STATE:] = jnp.broadcast_to(keep[...], (8, LANES))
        each_copy(g, lambda copy: copy.start(), lambda copy: None)

    @pl.when(phase == 1)
    def _():
        local_part(g, xs_s[g], dy, cols, rows_ref, gram, gram_t, y_out, u_out, dgram, g_s, gt_s)

    @pl.when((phase == 1) & (g == pairs - 1))
    def _():
        def join(pair, carry):
            each_copy(pair, lambda copy: copy.wait_send(), lambda copy: copy.wait_recv())
            sums = []
            for way in range(2):
                total = got[way, 0, pair, :STATE]
                decay = got[way, 0, pair, STATE : STATE + 1]
                for j in range(1, reach):
                    total = total + decay * got[way, j, pair, :STATE]
                    decay = decay * got[way, j, pair, STATE : STATE + 1]
                sums.append(total)
            entering[pair] = sums[0]
            leaving[pair] = sums[1]
            ending = fresh[pair, STATE : STATE + 1] * sums[0] + fresh[pair, :STATE]
            closing[pair] = jnp.sum(sums[1] * ending, axis=0, keepdims=True)
            return carry

        lax.fori_loop(0, pairs, join, 0)


def local_part(g, xs, dy, cols, rows_ref, gram, gram_t, y_out, u_out, dgram, g_s, gt_s):
    rows = dy.shape[0]
    blocks = rows // SUB
    half = rows // 2

    @pl.when(g == 0)
    def _():
        dgram[...] = jnp.zeros_like(dgram)
        g_s[0], g_s[1] = split(gram[...])
        gt_s[0], gt_s[1] = split(gram_t[...])

    columns = cols[0]
    lanes = first_lanes(SUB)
    zero = jnp.zeros((SUB, LANES), f32)
    grad = dy[...].astype(f32)
    for b in range(blocks):
        at = slice(b * SUB, (b + 1) * SUB)
        decays, m, mt = [], [], []
        for j in range(PAIR):
            down = columns[at, j : j + 1]
            across = rows_ref[0, j : j + 1, at]
            gap = down - across
            decay = jnp.exp2(jnp.minimum(gap, 0.0))
            decays.append(decay)
            m.append(gram[at, at] * decay)
            mt.append(gram_t[at, at] * jnp.exp2(jnp.minimum(-gap, 0.0)))
        mh, ml = split(jnp.concatenate(m, axis=1))
        mth, mtl = split(jnp.concatenate(mt, axis=1))
        xb = xs[at]
        high = xb.astype(bf16).astype(f32)
        low = xb - high
        xbh = jnp.concatenate([jnp.where(lanes, high, zero), jnp.where(lanes, zero, high)], axis=0).astype(bf16)
        xbl = jnp.concatenate([jnp.where(lanes, low, zero), jnp.where(lanes, zero, low)], axis=0).astype(bf16)
        gb = grad[at]
        gbd = jnp.concatenate([jnp.where(lanes, gb, zero), jnp.where(lanes, zero, gb)], axis=0).astype(bf16)
        both = mm(mh, jnp.concatenate([xbh, xbl], axis=1))
        y_out[at] = both[:, :LANES] + (both[:, LANES:] + mm(ml, xbh))
        u_out[at] = mm(mth, gbd) + mm(mtl, gbd)
        d = mm_nt(
            jnp.concatenate([gbd, gbd], axis=1),
            jnp.concatenate([high.astype(bf16), low.astype(bf16)], axis=1),
        )
        dgram[at, at] += d[:SUB] * decays[0] + d[SUB:] * decays[1]

    def across_blocks(low, mid, top, which):
        early, late = slice(low, mid), slice(mid, top)
        factor = spread(columns[low:top], which)
        size = mid - low
        fe, fl = factor[:size], factor[size:]
        source = split(fe * xs[early])
        target = split(fl * grad[late])
        y_out[late] += fl * mm3((g_s[0, late, early], g_s[1, late, early]), source)
        u_out[early] += fe * mm3((gt_s[0, early, late], gt_s[1, early, late]), target)
        dgram[late, early] += mm3_nt(target, source)

    for b in range(0, blocks, 2):
        across_blocks(b * SUB, (b + 1) * SUB, (b + 2) * SUB, C_NEAR)
    across_blocks(0, half, rows, C_FAR)


def final_kernel(
    pre_ref, x, rim, dy, cols, usable, taps, skip, projected, entering, leaving, y_in, u_in,
    mixed, vgrad, tail, rim_out, tap_grad, token_sums, skip_sums, dproj,
    pad, dpad, p_s,
):
    rows = dy.shape[0]

    @pl.when(pl.program_id(0) == 0)
    def _():
        dproj[...] = jnp.zeros_like(dproj)
        p_s[0], p_s[1] = split(projected[...])
        dpad[0:8] = jnp.zeros((8, LANES), f32)
        dpad[8 + rows : 16 + rows] = jnp.zeros((8, LANES), f32)

    write = (p_s[0, :, :STATE], p_s[1, :, :STATE])
    read = (p_s[0, :, STATE:], p_s[1, :, STATE:])
    columns = cols[0]
    pre = pre_ref[...]
    gate = sigmoid(pre)
    values = pre * gate
    step = spread(columns, C_STEP)
    grad = dy[...].astype(f32)
    ent = split(entering[0])
    lea = split(leaving[0])
    enter = spread(columns, C_ENTER)
    leave = spread(columns, C_LEAVE)
    y = y_in[...] + enter * mm3(read, ent)
    u = u_in[...] + leave * mm3(write, lea)
    dproj[:, STATE:] += mm3_nt(split(enter * grad), ent)
    dproj[:, :STATE] += mm3_nt(split(leave * step * values), lea)
    gain = skip[0:1, :]
    mixed[...] = (y + gain * values).astype(bf16)
    dvalues = step * u + gain * grad
    skip_sums[0] = jnp.broadcast_to(jnp.sum(grad * values, axis=0, keepdims=True), (8, LANES))
    lane = lax.broadcasted_iota(jnp.int32, (8, LANES), 1) // HEAD_DIM
    row = lax.broadcasted_iota(jnp.int32, (8, LANES), 0)
    chosen = jnp.where(row == lane, 1.0, 0.0).astype(bf16)
    chosen = jnp.concatenate([chosen, chosen], axis=1)
    first = mm_nt(chosen, jnp.concatenate(split(grad * y), axis=1))
    second = mm_nt(chosen, jnp.concatenate(split(values * u), axis=1))
    token_sums[0, 0:2] = first[0:2]
    token_sums[0, 2:4] = second[0:2]
    dpre = dvalues * (gate * (1.0 + pre * (1.0 - gate)))

    pad[0:8] = rim[...]
    pad[8 : 8 + rows] = x[...].astype(f32)
    total = jnp.zeros((rows + 8, LANES), f32)
    for k in range(KERNEL):
        part = dpre
        if k < KERNEL - 1:
            part = part * usable[:, k * LANES : (k + 1) * LANES]
        tap_grad[k : k + 1, :] = jnp.sum(part * pad[5 + k : 5 + k + rows], axis=0, keepdims=True)
        dpad[8 : 8 + rows] = part
        total = total + taps[k : k + 1, :] * dpad[3 - k + 0 : 3 - k + rows + 8]
    rim_out[...] = total[0:8]
    vgrad[...] = total[8:].astype(bf16)
    tail[...] = total[rows:]


def sum_kernel(
    groups, members, local_rows, part, small, state_out, small_out, cs_out,
    part_in, small_in, chunk, chunk_in, cs_in, send_p, recv_p, send_s, recv_s, send_c, recv_c, send_k, recv_k,
):
    ctx = lax.axis_size("ctx")
    me = lax.axis_index("head")
    mine = lax.axis_index("dp") * ctx + lax.axis_index("ctx")
    size = part.shape[0] // groups

    def along(offset):
        return {"head": lax.rem(me + offset, groups)}

    def beside(offset):
        other = lax.rem(mine + offset, members)
        return {"dp": other // ctx, "ctx": lax.rem(other, ctx)}

    def remote(src, dst, send, recv, device):
        return pltpu.make_async_remote_copy(
            src_ref=src, dst_ref=dst, send_sem=send, recv_sem=recv, device_id=device,
            device_id_type=pl.DeviceIdType.MESH,
        )

    barrier = pltpu.get_barrier_semaphore()
    for o in range(1, groups):
        pl.semaphore_signal(barrier, inc=1, device_id=along(o), device_id_type=pl.DeviceIdType.MESH)
    for o in range(1, members):
        pl.semaphore_signal(barrier, inc=1, device_id=beside(o), device_id_type=pl.DeviceIdType.MESH)
    pl.semaphore_wait(barrier, groups + members - 2)

    first = []
    for o in range(1, groups):
        to = lax.rem(me + o, groups)
        src = part.at[pl.ds(pl.multiple_of(to * size, size), size)]
        first.append(remote(src, part_in.at[o - 1], send_p.at[o - 1], recv_p.at[o - 1], along(o)))
    for o in range(1, members):
        first.append(remote(small, small_in.at[o - 1], send_s.at[o - 1], recv_s.at[o - 1], beside(o)))
    for copy in first:
        copy.start()
    for copy in first:
        copy.wait()

    total = part[pl.ds(pl.multiple_of(me * size, size), size), :]
    for o in range(1, groups):
        total = total + part_in[o - 1]
    chunk[...] = total.astype(bf16)

    def in_order(own, slots, place, count):
        result = None
        for s in range(count):
            slot = jnp.maximum(lax.rem(place - s + count, count) - 1, 0)
            term = jnp.where(place == s, own, slots[slot])
            result = term if result is None else result + term
        return result

    summed = in_order(small[...], small_in, mine, members)
    small_out[...] = summed[:local_rows]
    cs_out[...] = summed[local_rows:]
    second = []
    for o in range(1, groups):
        second.append(remote(chunk, chunk_in.at[o - 1], send_c.at[o - 1], recv_c.at[o - 1], along(o)))
        second.append(remote(cs_out, cs_in.at[o - 1], send_k.at[o - 1], recv_k.at[o - 1], along(o)))
    for copy in second:
        copy.start()
    state_out[pl.ds(pl.multiple_of(me * size, size), size), :] = chunk[...]
    for copy in second:
        copy.wait()
    for o in range(1, groups):
        origin = lax.rem(me - o + groups, groups)
        state_out[pl.ds(pl.multiple_of(origin * size, size), size), :] = chunk_in[o - 1]
    cs_out[...] = in_order(cs_out[...], cs_in, me, groups)


def sum_across(part, small, local_rows):
    groups = lax.axis_size("head")
    members = lax.axis_size("dp") * lax.axis_size("ctx")
    rows, width = part.shape
    extra = small.shape[0] - local_rows
    size = rows // groups
    vmem = pl.BlockSpec(memory_space=pltpu.VMEM)
    dma = pltpu.SemaphoreType.DMA
    return pl.pallas_call(
        partial(sum_kernel, groups, members, local_rows),
        in_specs=[vmem, vmem],
        out_specs=[vmem, vmem, vmem],
        out_shape=[jax.ShapeDtypeStruct((rows, width), bf16), jax.ShapeDtypeStruct((local_rows, 128), f32),
                   jax.ShapeDtypeStruct((extra, 128), f32)],
        scratch_shapes=[
            pltpu.VMEM((groups - 1, size, width), f32),
            pltpu.VMEM((members - 1, *small.shape), f32),
            pltpu.VMEM((size, width), bf16),
            pltpu.VMEM((groups - 1, size, width), bf16),
            pltpu.VMEM((groups - 1, extra, 128), f32),
            dma((groups - 1,)), dma((groups - 1,)), dma((members - 1,)), dma((members - 1,)),
            dma((groups - 1,)), dma((groups - 1,)), dma((groups - 1,)), dma((groups - 1,)),
        ],
        compiler_params=pltpu.CompilerParams(
            collective_id=0, has_side_effects=True, vmem_limit_bytes=32 * 1024 * 1024
        ),
        name="sums",
    )(part, small)


def on_device(
    value_input,
    state_proj,
    step_raw,
    doc_lengths,
    conv_value,
    conv_state,
    step_bias,
    decay_log,
    skip_gain,
    out_grad,
):
    rows, channels = value_input.shape[1:]
    heads = step_raw.shape[1]
    pairs = heads // PAIR
    blocks = rows // SUB
    half = rows // 2
    rim = KERNEL - 1
    ctx_place = lax.axis_index("ctx")
    context_count = lax.axis_size("ctx")
    whole = rows * context_count
    reach = min(context_count - 1, (whole // 2 - 2) // rows + 1)
    dev_start = ctx_place * rows
    positions = dev_start + jnp.arange(rows, dtype=jnp.int32)
    starts = token_starts(doc_lengths[0], positions)
    x = value_input[0]
    dy = out_grad[0]
    tail_rows = rows - rim
    rims = shifted(jnp.concatenate([x[tail_rows:], state_proj[0, tail_rows:]], axis=1), "ctx", 1)
    value_rim = jnp.concatenate([jnp.zeros((8 - rim, channels), f32), rims[:, :channels].astype(f32)], axis=0)
    state_rim = rims[:, channels:].astype(f32)

    usable = [(positions - rim + k >= starts).astype(f32) for k in range(KERNEL)]
    usable_wide = jnp.concatenate(
        [jnp.broadcast_to(usable[k][:, None], (rows, LANES)) for k in range(rim)], axis=1
    )
    projected, state_pullback = jax.vjp(
        lambda series, weights, rim_rows: causal_conv(series, weights, usable, rim_rows),
        state_proj[0].astype(f32), conv_state, state_rim,
    )
    write_rows, read_rows = projected[:, :STATE], projected[:, STATE:]
    allowed = (positions[None, :] <= positions[:, None]) & (positions[None, :] >= starts[:, None])
    gram = jnp.where(allowed, jnp.dot(read_rows, write_rows.T, precision=precise), 0.0)
    gram_t = jnp.where(allowed.T, jnp.dot(write_rows, read_rows.T, precision=precise), 0.0)

    logits = step_raw[0] + step_bias[:, None]
    step = jax.nn.softplus(logits)
    rate = jnp.exp(decay_log)[:, None]
    log_decay = -rate * step
    index = jnp.arange(SUB)
    upper = (index[:, None] <= index[None, :]).astype(f32)
    cum = jnp.einsum("hbs,st->hbt", log_decay.reshape(heads, blocks, SUB), upper, precision=precise)
    totals = cum[:, :, -1]

    def flat(value):
        return value.reshape(heads, rows)

    def before(first, block):
        return sum((totals[:, i] for i in range(first, block)), jnp.zeros((heads,), f32))

    near, far, enter, leave = [], [], [], []
    for b in range(blocks):
        inner = cum[:, b]
        rest = totals[:, b : b + 1] - inner
        near.append(inner if b % 2 else rest)
        if b >= blocks // 2:
            far.append(inner + before(blocks // 2, b)[:, None])
        else:
            far.append(rest + before(b + 1, blocks // 2)[:, None])
        enter.append(inner + before(0, b)[:, None])
        leave.append(rest + before(b + 1, blocks)[:, None])
    near, far, enter, leave = (jnp.exp(jnp.concatenate(v, axis=1)) for v in (near, far, enter, leave))
    enter = enter * (starts < dev_start).astype(f32)[None]
    leave = leave * (positions >= starts[-1]).astype(f32)[None]
    keep = jnp.exp(before(0, blocks)) * (starts[-1] < dev_start).astype(f32)
    cum2 = flat(cum) * LOG2E
    cols = jnp.stack([cum2, step, near, far, enter, leave])
    cols = cols.reshape(6, pairs, PAIR, rows).transpose(1, 3, 0, 2).reshape(pairs, rows, 6 * PAIR)
    row_form = cum2.reshape(pairs, PAIR, rows)

    col_spec = pl.BlockSpec((rows, LANES), lambda g: (0, g))
    cols_spec = pl.BlockSpec((1, rows, 6 * PAIR), lambda g: (g, 0, 0))
    eight_spec = pl.BlockSpec((8, LANES), lambda g: (0, g))
    taps_spec = pl.BlockSpec((KERNEL, LANES), lambda g: (0, g))
    state_spec = pl.BlockSpec((1, STATE, LANES), lambda g: (g, 0, 0))

    def wide(value):
        return jnp.repeat(value, HEAD_DIM)[None, :]

    def fixed(*shape):
        return pl.BlockSpec(shape, lambda g: (0,) * len(shape))

    def like(*shape, dtype=f32):
        return jax.ShapeDtypeStruct(shape, dtype)

    params = pltpu.CompilerParams(
        dimension_semantics=("arbitrary",), vmem_limit_bytes=48 * 1024 * 1024
    )
    def early(*shape):
        return pl.BlockSpec(shape, lambda p, g: (0, jnp.where(p == 0, g, pairs - 1)))

    def late(*shape):
        return pl.BlockSpec(shape, lambda p, g: (0, jnp.where(p == 0, 0, g)))

    def always(*shape):
        return pl.BlockSpec(shape, lambda p, g: (0,) * len(shape))

    sent = (STATE + 8, LANES)
    pre, y_local, u_local, dgram, entering, leaving, closing = pl.pallas_call(
        partial(start_kernel, reach),
        grid=(2, pairs),
        in_specs=[early(rows, LANES), early(8, LANES), pl.BlockSpec((rows, LANES), lambda p, g: (0, g)),
                  early(KERNEL, LANES), always(rows, rim * LANES),
                  pl.BlockSpec((1, rows, 6 * PAIR), lambda p, g: (g, 0, 0)), always(rows, 2 * STATE),
                  early(1, LANES), pl.BlockSpec((1, PAIR, rows), lambda p, g: (g, 0, 0)),
                  always(rows, rows), always(rows, rows)],
        out_specs=[early(rows, LANES), late(rows, LANES), late(rows, LANES), always(rows, rows),
                   always(pairs, STATE, LANES), always(pairs, STATE, LANES), always(pairs, 1, LANES)],
        out_shape=[like(rows, channels), like(rows, channels), like(rows, channels), like(rows, rows),
                   like(pairs, STATE, LANES), like(pairs, STATE, LANES), like(pairs, 1, LANES)],
        scratch_shapes=[
            pltpu.VMEM((rows + 8, LANES), f32), pltpu.VMEM((2, STATE, rows), bf16),
            pltpu.VMEM((2, STATE, rows), bf16), pltpu.VMEM((2, rows, rows), bf16),
            pltpu.VMEM((2, rows, rows), bf16), pltpu.VMEM((pairs, rows, LANES), f32),
            pltpu.VMEM((pairs, *sent), f32), pltpu.VMEM((pairs, *sent), f32),
            pltpu.VMEM((2, reach, pairs, *sent), f32),
            pltpu.SemaphoreType.DMA((2, reach, pairs)), pltpu.SemaphoreType.DMA((2, reach, pairs)),
        ],
        compiler_params=pltpu.CompilerParams(
            dimension_semantics=("arbitrary", "arbitrary"), vmem_limit_bytes=52 * 1024 * 1024,
            collective_id=1, has_side_effects=True,
        ),
        name="start",
    )(x, value_rim, dy, conv_value, usable_wide, cols, projected, wide(keep), row_form, gram, gram_t)

    mixed, vgrad, tail, rim_grad, tap_grad, token_sums, skip_sums, dproj = pl.pallas_call(
        final_kernel,
        grid=(pairs,),
        in_specs=[col_spec, col_spec, eight_spec, col_spec, cols_spec, fixed(rows, rim * LANES), taps_spec,
                  pl.BlockSpec((1, LANES), lambda g: (0, g)), fixed(rows, 2 * STATE), state_spec, state_spec,
                  col_spec, col_spec],
        out_specs=[col_spec, col_spec, eight_spec, eight_spec, taps_spec,
                   pl.BlockSpec((1, 2 * PAIR, rows), lambda g: (g, 0, 0)),
                   pl.BlockSpec((1, 8, LANES), lambda g: (g, 0, 0)), fixed(rows, 2 * STATE)],
        out_shape=[like(rows, channels, dtype=bf16), like(rows, channels, dtype=bf16), like(8, channels),
                   like(8, channels), like(KERNEL, channels), like(pairs, 2 * PAIR, rows),
                   like(pairs, 8, LANES), like(rows, 2 * STATE)],
        scratch_shapes=[pltpu.VMEM((rows + 8, LANES), f32), pltpu.VMEM((rows + 16, LANES), f32),
                        pltpu.VMEM((2, rows, 2 * STATE), bf16)],
        compiler_params=params,
        name="final",
    )(pre, x, value_rim, dy, cols, usable_wide, conv_value, wide(skip_gain), projected, entering, leaving,
      y_local, u_local)

    dgram = jnp.where(allowed, dgram, 0.0)
    dread = jnp.dot(dgram, write_rows, precision=precise)
    dwrite = jnp.dot(dgram.T, read_rows, precision=precise)
    dprojected = dproj + jnp.concatenate([dwrite, dread], axis=1)
    dstate, dconv_state, dstate_rim = state_pullback(dprojected)

    sums = token_sums.reshape(pairs, 2, PAIR, rows)
    out_dot = sums[:, 0].reshape(heads, rows)
    in_dot = sums[:, 1].reshape(heads, rows)
    closing = jnp.sum(closing.reshape(heads, HEAD_DIM), axis=1)
    dcum = out_dot - step * in_dot
    order = jnp.arange(rows)
    later = (order[:, None] >= order[None, :]).astype(f32)
    dlog = jnp.dot(dcum, later, precision=precise) + closing[:, None]
    dstep = in_dot - rate * dlog
    step_grad = dstep * jax.nn.sigmoid(logits)
    head_part = jnp.stack([
        jnp.sum(step_grad, axis=1),
        jnp.sum(dlog * log_decay, axis=1),
        jnp.sum(skip_sums[:, 0].reshape(heads, HEAD_DIM), axis=1),
    ])

    rims_back = shifted(jnp.concatenate([rim_grad[8 - rim :], dstate_rim], axis=1), "ctx", -1)
    tail_total = tail.at[8 - rim :].add(rims_back[:, :channels])
    value_grad = lax.dynamic_update_slice(vgrad, tail_total.astype(bf16), (rows - 8, 0))
    state_partial = dstate.at[tail_rows:].add(rims_back[:, channels:])
    tap_rows = KERNEL * channels // 128
    head_flat = jnp.pad(head_part.reshape(-1), (0, 8 * 128 - 3 * heads)).reshape(8, 128)
    small = jnp.concatenate([tap_grad.reshape(tap_rows, 128), head_flat, dconv_state.reshape(-1, 128)])
    state_grad, small_sum, conv_state_sum = sum_across(state_partial, small, tap_rows + 8)
    conv_value_grad = small_sum[:tap_rows].reshape(KERNEL, channels)
    head_grads = small_sum[tap_rows:].reshape(-1)[: 3 * heads].reshape(3, heads)
    conv_state_grad = conv_state_sum.reshape(KERNEL, 2 * STATE)
    return (
        mixed[None],
        value_grad[None],
        state_grad[None],
        step_grad[None],
        conv_value_grad,
        conv_state_grad,
        head_grads,
    )


def solution(mesh):
    return jax.shard_map(
        on_device,
        mesh=mesh,
        in_specs=(
            P("dp", "ctx", "head"),
            P("dp", "ctx", None),
            P("dp", "head", "ctx"),
            P("dp", None),
            P(None, "head"),
            P(),
            P("head"),
            P("head"),
            P("head"),
            P("dp", "ctx", "head"),
        ),
        out_specs=(
            P("dp", "ctx", "head"),
            P("dp", "ctx", "head"),
            P("dp", "ctx", None),
            P("dp", "head", "ctx"),
            P(None, "head"),
            P(),
            P(None, "head"),
        ),
        check_vma=False,
    )
```
